128 devices in a mesh: expert: 8 (over z, y_lo), replica: 16 (over x, y_hi, core).
Axes of the slice: x: 4, y: 4 (y_hi: 2, y_lo: 2; y = y_hi * 2 + y_lo), z: 4, core: 2. Of those that a mesh axis runs over, the one named last changes fastest.
Arguments:
- tokens: bfloat16 [16384, 3584], P(('expert', 'replica')), may hold values from -6 to 6
- routes: int32 [16384, 2], P(('expert', 'replica')), may hold values from 0 to 7, all different within a row; in each aligned block of 128 rows (0 to 127, 128 to 255, ...) at most 64 rows name the same one
- cotangent: bfloat16 [16384, 2, 1280], P(('expert', 'replica')), may hold values from -0.08984375 to 0.08984375
- weights: bfloat16 [8, 3584, 1280], P('expert', 'replica'), may hold values from -0.09375 to 0.09375
- first_moment: float32 [8, 3584, 1280], P('expert', 'replica'), may hold values from -6 to 6
- second_moment: float32 [8, 3584, 1280], P('expert', 'replica'), may hold values from 0.25 to 4
- pairing: int32 [8], replicated, may hold values from 0 to 7, as said below
Outputs:
- activation: bfloat16 [16384, 2, 1280], P(('expert', 'replica'))
- new_weights: bfloat16 [8, 3584, 1280], P('expert', 'replica')
- new_first: float32 [8, 3584, 1280], P('expert', 'replica')
- new_second: float32 [8, 3584, 1280], P('expert', 'replica')
- update: float32 [8, 3584, 1280], P('expert', 'replica')
The draws below stay inside these ranges and needn't reach their ends.
Inputs may be any that keep to these rules, and one draw needn't show every extreme that they name: `routes`: each row names 2 different experts. Within the rows of one device no expert is named by more than 64 rows, and in every draw some device names some expert in exactly 64 rows. The experts fall into pairs: pairing[pairing[s]] == s and pairing[s] != s for every s.
All inputs are finite; a program needn't handle non-finite values.
Results may differ from the reference program's by a relative error of at most 0.0045.
Values may be sent and summed in bfloat16 or wider, within the bound.
A program may use at most 128 MiB of HBM per device.

```python
import math
import jax
import jax.numpy as jnp
import numpy as np
from jax import lax

D = 3584
FW = 1280
TOP = 2
TOK_DEV = 128
EXPERTS = 8
CAP = 64
TOKENS = 16384
N_EXPERT = 8
N_REPLICA = 16


def draw_pairing(key, part):
    order = jax.random.permutation(key, EXPERTS).astype(jnp.int32)
    evens = order[0::2]
    odds = order[1::2]
    return jnp.zeros((EXPERTS,), jnp.int32).at[evens].set(odds).at[odds].set(evens)


def levels(stream_key, shape, pieces, least, largest):
    level, own = 1.0, jax.random.fold_in(stream_key, 6)
    for position, shards_of in pieces:
        steps = jnp.exp(jax.random.uniform(jax.random.fold_in(own, position), (shards_of,), jnp.float32, least / len(pieces), largest / len(pieces)))
        level = level * jnp.repeat(steps, shape[position] // shards_of).reshape([-1 if axis == position else 1 for axis in range(len(shape))])
    return level


def deal_out(own_key, own, number, rows, count, top, most, slope):
    order = jax.random.permutation(own_key, count)
    packed, usual = portions_of(count, rows * top, most, slope, True), portions_of(count, rows * top, most, slope, False)
    places = jnp.arange(count)

    def named(sizes, rotation):
        used = int((sizes > 0).sum())
        fixed = max(1, used // 4)
        shifted = fixed + (places - fixed + rotation * (used - fixed)) % max(1, count - fixed)
        return jnp.zeros((count,), jnp.int32).at[order[jnp.where(places < fixed, places, shifted)]].set(jnp.asarray(sizes, jnp.int32))

    sizes = jnp.where(number % 4 == 0, named(packed, number // 4), named(usual, number - number // 4 - 1))
    mixed = jax.random.permutation(jax.random.fold_in(own, 3), count)
    source_of, sink = mixed[0:count // 2 * 2:2], mixed[1:count // 2 * 2:2]
    slack = jnp.minimum(sizes[source_of] - 1, most - sizes[sink]) // 2
    slack = jnp.where((source_of == order[0]) | (sink == order[0]) | (sizes[sink] == 0), 0, jnp.maximum(slack, 0))
    shifted = jax.random.randint(jax.random.fold_in(own, 4), (count // 2,), 0, 1 << 20) % (slack + 1)
    sizes = sizes.at[source_of].add(-shifted).at[sink].add(shifted)
    labels = jnp.searchsorted(jnp.cumsum(sizes), jnp.arange(rows * top), side="right").astype(jnp.int32)
    grid = labels.reshape(top, rows).T
    grid = grid[jax.random.permutation(jax.random.fold_in(own, 1), rows)]
    rotation = jax.random.randint(jax.random.fold_in(own, 2), (rows, 1), 0, top)
    return jnp.take_along_axis(grid, (jnp.arange(top)[None, :] + rotation) % top, axis=1)


def portions_of(number_of, total, limit, slope, full):
    portions = [(1 << 20) // math.isqrt(standing ** slope) + 1 for standing in range(1, number_of + 1)]
    largest = limit if full else min(limit, max(-(-total // number_of), total * portions[0] // sum(portions)))
    least = 1 if total - largest >= number_of - 1 else 0
    given, rest = [largest] + [least] * (number_of - 1), total - largest - least * (number_of - 1)
    while rest > 0:
        free = [i for i in range(1, number_of) if given[i] < largest] or [i for i in range(1, number_of) if given[i] < limit]
        whole, left = sum([portions[i] for i in free]), rest
        for i in free:
            addition = min(limit - given[i], max(1, left * portions[i] // whole), rest)
            given[i] = given[i] + addition
            rest = rest - addition
    return np.array(given)


def normal_values(rng, dims, deviation, limit, split=(), kind=jnp.bfloat16):
    drawn = deviation * jax.random.normal(rng, dims, jnp.float32)
    if split:
        drawn = drawn * levels(rng, dims, split, -0.22, 0.18)
    return jnp.clip(drawn, -limit, limit).astype(kind)


def setup_inputs(seed: int = 0) -> dict:
    seeds = jax.random.split(jax.random.key(seed), 8)
    tokens = normal_values(seeds[0], (TOKENS, D), 1.0, 6.0, ((0, 128),))
    routes_keys = jax.random.split(jax.random.fold_in(seeds[1], 1), TOKENS // TOK_DEV)
    routes_turns = jax.random.permutation(jax.random.fold_in(seeds[1], 3), TOKENS // TOK_DEV)
    routes = jax.vmap(lambda own, number: deal_out(jax.random.fold_in(seeds[1], 2), own, number, TOK_DEV, EXPERTS, TOP, CAP, 2))(routes_keys, routes_turns).reshape((TOKENS, TOP))
    cotangent = normal_values(seeds[2], (TOKENS, TOP, FW), 0.015625, 0.08984375, ((0, 128),))
    weights = normal_values(seeds[3], (EXPERTS, D, FW), D ** -0.5, 0.09375, ((0, 8), (1, 16)))
    first_moment = normal_values(seeds[4], (EXPERTS, D, FW), 1.0, 6.0, ((0, 8), (1, 16)), jnp.float32)
    second_moment = jnp.clip(jnp.exp(math.log(4.0) - 2.7725887 * jax.random.uniform(seeds[5], (EXPERTS, D, FW), jnp.float32) ** levels(seeds[5], (EXPERTS, D, FW), ((0, 8), (1, 16)), -0.2, 0.2)), 0.25, 4.0)
    pairing = draw_pairing(jax.random.fold_in(seeds[7], 71), 0)
    return dict(tokens=tokens, routes=routes, cotangent=cotangent, weights=weights, first_moment=first_moment, second_moment=second_moment, pairing=pairing)


BETA_ONE = 0.8
BETA_TWO = 0.9
EPSILON = 1e-08

def reference(tokens, routes, cotangent, weights, first_moment, second_moment, pairing):
    group_tokens = N_EXPERT * TOK_DEV
    route_count = group_tokens * TOP
    bucket = N_EXPERT * CAP
    token_blocks = tokens.reshape(N_EXPERT, N_REPLICA, TOK_DEV, D).transpose(1, 0, 2, 3)
    route_blocks = routes.reshape(N_EXPERT, N_REPLICA, TOK_DEV, TOP).transpose(1, 0, 2, 3)
    grad_blocks = cotangent.reshape(N_EXPERT, N_REPLICA, TOK_DEV, TOP, FW).transpose(1, 0, 2, 3, 4)
    expert_ids = jnp.arange(EXPERTS, dtype=jnp.int32)

    def one_expert(operands):
        expert_rows, expert_grads, expert_weight = operands
        projected = jnp.dot(expert_rows, expert_weight, preferred_element_type=jnp.float32)
        partial_value = jnp.dot(expert_rows.T, expert_grads, preferred_element_type=jnp.float32)
        return (projected.astype(jnp.bfloat16), partial_value.astype(jnp.bfloat16))

    def one_group(running, group):
        group_rows, group_routes, group_grads = group
        group_rows = group_rows.reshape(group_tokens, D)
        flat_routes = group_routes.reshape(route_count).astype(jnp.int32)
        flat_grads = group_grads.reshape(route_count, FW)
        one_hot = (flat_routes[:, None] == expert_ids[None, :]).astype(jnp.int32)
        places = lax.optimization_barrier(jnp.sum((jnp.cumsum(one_hot, axis=0) - 1) * one_hot, axis=1)).astype(jnp.int32)
        table = jnp.full((EXPERTS, bucket), route_count, jnp.int32)
        table = table.at[flat_routes, places].set(jnp.arange(route_count, dtype=jnp.int32))
        token_index = jnp.where(table < route_count, table // TOP, group_tokens).astype(jnp.int32)
        padded_rows = jnp.concatenate([group_rows, jnp.zeros((1, D), group_rows.dtype)], axis=0)
        padded_grads = jnp.concatenate([flat_grads, jnp.zeros((1, FW), flat_grads.dtype)], axis=0)
        projected, partial_value = lax.map(one_expert, (padded_rows[token_index], padded_grads[table], weights))
        activation = projected[flat_routes, places].reshape(N_EXPERT, TOK_DEV, TOP, FW)
        partial_value = lax.optimization_barrier(partial_value)
        return (running + partial_value.astype(jnp.float32), activation)
    start = jnp.zeros((EXPERTS, D, FW), jnp.float32)
    gradient, activation = lax.scan(one_group, start, (token_blocks, route_blocks, grad_blocks))
    activation = activation.transpose(1, 0, 2, 3, 4).reshape(TOKENS, TOP, FW)
    new_weights = weights[pairing]
    moved_grad = gradient[pairing]
    new_first = BETA_ONE * first_moment[pairing] + (1.0 - BETA_ONE) * moved_grad
    new_second = BETA_TWO * second_moment[pairing] + (1.0 - BETA_TWO) * moved_grad * moved_grad
    update = new_first / (jnp.sqrt(new_second) + EPSILON)
    return (activation, new_weights, new_first, new_second, update)
```

```python
import jax
import jax.numpy as jnp
from jax import lax
from jax.experimental import pallas as pl
from jax.experimental.pallas import tpu as pltpu
from jax.sharding import PartitionSpec as P

BETA_ONE = 0.8
BETA_TWO = 0.9
EPSILON = 1e-08
MESH = pl.DeviceIdType.MESH
BF = jnp.bfloat16
F32 = jnp.float32

D, FW, TOK, CAP, NE, SHARD, CHUNK = 3584, 1280, 128, 64, 8, 224, 896
ROWS = NE * CAP
TILE = 256


def kernel(
    pair, rt, tok, cot, w, m1, m2,
    act, wn, m1n, m2n, g,
    w1, w2s, wfull, b1s, b1r, b2s, b2r, tp, tr, cp, cr, acc, ps, pr, part, sibr, xr, yr, g0, g1,
    s_m, s_w1, r_w1, s_w2, r_w2, s_b1, r_b1, s_b2, r_b2, s_t, r_t, s_c, r_c, s_e, r_e,
    s_ag, r_ag, s_sb, r_sb, s_x, r_x, s_y, r_y,
):
    e = lax.axis_index("expert")
    r = lax.axis_index("replica")
    x = r // 4
    yh = (r // 2) % 2
    c = r % 2

    def rid(x_, yh_, c_):
        return x_ * 4 + yh_ * 2 + c_

    xp, xm, xo = (x + 1) % 4, (x + 3) % 4, (x + 2) % 4
    sib = (e, rid(x, yh, 1 - c))
    yp = (e, rid(x, 1 - yh, c))
    px = (e, rid(xp, yh, c))
    mx = (e, rid(xm, yh, c))

    def rc(src, dst, ss, rs, dev):
        return pltpu.make_async_remote_copy(
            src_ref=src, dst_ref=dst, send_sem=ss, recv_sem=rs, device_id=dev, device_id_type=MESH
        )

    def got(ref, sem):
        rc(ref, ref, sem, sem, sib).wait_recv()

    def gone(ref, sem):
        rc(ref, ref, sem, sem, sib).wait_send()

    loads = [
        pltpu.make_async_copy(m1, acc.at[pl.ds(0, SHARD)], s_m.at[0]),
        pltpu.make_async_copy(m2, acc.at[pl.ds(SHARD, SHARD)], s_m.at[1]),
    ]
    for load in loads:
        load.start()

    barrier = pltpu.get_barrier_semaphore()

    @pl.loop(1, NE)
    def _(d):
        pl.semaphore_signal(barrier, inc=1, device_id=((e + d) % NE, r), device_id_type=MESH)

    for dev in (sib, yp, px, mx):
        pl.semaphore_signal(barrier, inc=1, device_id=dev, device_id_type=MESH)
    pl.semaphore_wait(barrier, NE - 1 + 4)

    @pl.loop(0, 7)
    def _(i):
        rows = pl.ds(pl.multiple_of(i * 32, 32), 32)

        @pl.when(i != e)
        def _():
            rc(w.at[rows], w1.at[e], s_w1.at[i], r_w1.at[e], (i, r)).start()

        @pl.when(i == e)
        def _():
            w1[e] = w[rows, :]

    owners = []
    for k in range(2):
        row = rt[k : k + 1, :]
        own = jnp.zeros_like(row)
        for s in range(NE):
            own = own + jnp.where(row == s, pair[s], 0)
        owners.append(own)
    places = lax.broadcasted_iota(jnp.int32, (NE, TOK), 0)
    named = [(places == own) for own in owners]
    mask = jnp.where(named[0] | named[1], 1.0, 0.0)
    earlier = jnp.where(
        lax.broadcasted_iota(jnp.int32, (TOK, TOK), 0) < lax.broadcasted_iota(jnp.int32, (TOK, TOK), 1), 1.0, 0.0
    )
    rank = jnp.dot(mask.astype(BF), earlier.astype(BF), preferred_element_type=F32)
    slots = lax.broadcasted_iota(jnp.int32, (ROWS, TOK), 0).astype(F32)
    for k, ref in ((0, g0), (1, g1)):
        slot = jnp.sum(jnp.where(named[k], rank, 0.0), axis=0, keepdims=True) + owners[k].astype(F32) * CAP
        ref[...] = jnp.where(slots == slot, 1.0, 0.0).astype(BF)

    @pl.loop(0, FW // TILE)
    def _(n):
        a = jnp.dot(g0[...], cot[:, pl.ds(pl.multiple_of(n * TILE, TILE), TILE)], preferred_element_type=F32)
        b = jnp.dot(g1[...], cot[:, pl.ds(pl.multiple_of(FW + n * TILE, TILE), TILE)], preferred_element_type=F32)
        cp[:, :, pl.ds(pl.multiple_of(n * TILE, TILE), TILE)] = (a + b).astype(BF).reshape(NE, CAP, TILE)

    @pl.when(e < 7)
    def _():
        @pl.loop(0, NE)
        def _(s):
            @pl.when(s != e)
            def _():
                got(w1.at[s], r_w1.at[s])

        rows = pl.ds(pl.multiple_of(e * 32, 32), 32)

        @pl.loop(0, NE)
        def _(s):
            v = w1[pair[s]]
            w2s[s] = v

            @pl.when(s != e)
            def _():
                rc(w2s.at[s], wfull.at[r, rows], s_w2.at[s], r_w2.at[e], (s, r)).start()

            @pl.when(s == e)
            def _():
                wfull[r, rows, :] = v

    def spread(src, dst, ss, rs):
        @pl.loop(1, NE)
        def _(d):
            s = (e + d) % NE
            rc(src(s), dst(e), ss(s), rs(e), (s, r)).start()

    spread(lambda s: cp.at[s], lambda s: cr.at[s], lambda s: s_c.at[s], lambda s: r_c.at[s])
    cr[e] = cp[e]

    order = (xo, xp, xm, x)
    for q in order[:2]:
        send_chunk(q, e, r, tok, g0, g1, tp, tr, s_t, r_t, spread)

    @pl.loop(0, 7)
    def _(i):
        @pl.when(i != e)
        def _():
            got(wfull.at[r, pl.ds(pl.multiple_of(i * 32, 32), 32)], r_w2.at[i])

    def ag(shard, k, dev):
        rc(wfull.at[shard], wfull.at[shard], s_ag.at[k], r_ag.at[shard], dev).start()

    ag(r, 0, yp)
    ag(r, 1, px)
    ag(r, 2, mx)
    ag(r, 3, sib)

    for q in order[2:]:
        send_chunk(q, e, r, tok, g0, g1, tp, tr, s_t, r_t, spread)

    for load in loads:
        load.wait()

    @pl.loop(0, NE)
    def _(p):
        rows = pl.ds(pl.multiple_of((p // 4) * SHARD + ((p // 2) % 2) * 112, 8), 112)
        cols = pl.ds(pl.multiple_of((p % 2) * 640, 128), 640)
        b1s[p] = acc[rows, cols].astype(BF)

        @pl.when(p != e)
        def _():
            rc(b1s.at[p], b1r.at[e], s_b1.at[p], r_b1.at[e], (p, r)).start()

        @pl.when(p == e)
        def _():
            b1r[e] = b1s[p]

    wn[...] = wfull[r]

    @pl.loop(1, NE)
    def _(d):
        s = (e + d) % NE
        got(cr.at[s], r_c.at[s])

    def wgrad(q):
        @pl.loop(1, NE)
        def _(d):
            s = (e + d) % NE
            got(tr.at[q, s], r_t.at[q, s])

        @pl.loop(0, FW // TILE)
        def _(n):
            cols = pl.ds(pl.multiple_of(n * TILE, TILE), TILE)
            v = lax.dot_general(
                tr[q].reshape(ROWS, CHUNK), cr[:, :, cols].reshape(ROWS, TILE), (((0,), (0,)), ((), ())),
                preferred_element_type=F32,
            )
            part[pl.ds(q * 4, 4), :, cols] = v.astype(BF).reshape(4, SHARD, TILE)

    def add(shard, other):
        @pl.loop(0, 7)
        def _(i):
            rows = pl.ds(pl.multiple_of(i * 32, 32), 32)
            part[shard, rows, :] = (part[shard, rows, :].astype(F32) + other[rows, :].astype(F32)).astype(BF)

    def to_sib(k, q):
        for h in range(2):
            rc(part.at[rid(q, h, 1 - c)], sibr.at[2 * k + h], s_sb.at[2 * k + h], r_sb.at[2 * k + h], sib).start()

    def from_sib(k, q):
        for h in range(2):
            got(sibr.at[2 * k + h], r_sb.at[2 * k + h])
            add(rid(q, h, c), sibr.at[2 * k + h])

    def xs(shard, slot, dev):
        rc(part.at[shard], xr.at[slot], s_x.at[slot], r_x.at[slot], dev).start()

    wgrad(xo)
    to_sib(0, xo)
    from_sib(0, xo)
    xs(rid(xo, 0, c), 0, px)
    xs(rid(xo, 1, c), 1, mx)

    def from_x(h, k):
        low, high = rid(xm, h, c), rid(xp, h, c)
        got(wfull.at[low], r_ag.at[low])
        ag(low, k, sib)
        got(wfull.at[high], r_ag.at[high])
        ag(high, k + 1, sib)
        ag(rid((x + 3 + 2 * h) % 4, h, c), k + 2, (e, rid((x + 1 + 2 * h) % 4, yh, c)))

    partner = rid(x, 1 - yh, c)
    got(wfull.at[partner], r_ag.at[partner])
    ag(partner, 4, px)
    ag(partner, 5, mx)
    ag(partner, 6, sib)
    from_x(yh, 7)

    wgrad(xp)
    to_sib(1, xp)
    from_sib(1, xp)
    xs(rid(xp, 1, c), 3, px)
    got(xr.at[0], r_x.at[0])
    add(rid(xp, 0, c), xr.at[0])
    xs(rid(xp, 0, c), 2, px)

    wgrad(xm)
    to_sib(2, xm)
    from_sib(2, xm)
    xs(rid(xm, 0, c), 5, mx)
    got(xr.at[1], r_x.at[1])
    add(rid(xm, 1, c), xr.at[1])
    xs(rid(xm, 1, c), 4, mx)

    @pl.loop(1, NE)
    def _(d):
        s = (e + d) % NE
        got(b1r.at[s], r_b1.at[s])

    @pl.loop(0, NE)
    def _(s):
        v = b1r[pair[s]]
        b2s[s] = v

        @pl.when(s != e)
        def _():
            rc(b2s.at[s], b2r.at[e], s_b2.at[s], r_b2.at[e], (s, r)).start()

        @pl.when(s == e)
        def _():
            b2r[e] = v

    from_x(1 - yh, 10)

    wgrad(x)
    to_sib(3, x)
    from_sib(3, x)

    def project(q, first):
        @pl.loop(0, FW // TILE)
        def _(n):
            cols = pl.ds(pl.multiple_of(n * TILE, TILE), TILE)
            v = jnp.dot(
                tr[q].reshape(ROWS, CHUNK), wfull[pl.ds(q * 4, 4), :, cols].reshape(CHUNK, TILE),
                preferred_element_type=F32,
            )
            if first:
                acc[:, cols] = v
            else:
                acc[:, cols] += v

    def sib_has(q):
        for h in range(2):
            shard = rid(q, h, 1 - c)
            got(wfull.at[shard], r_ag.at[shard])

    sib_has(x)
    project(x, True)
    sib_has(xp)
    project(xp, False)
    sib_has(xm)
    project(xm, False)
    far = (rid(xo, yh, c), rid(xo, 1 - yh, c))
    for k in range(2):
        got(wfull.at[far[k]], r_ag.at[far[k]])
        ag(far[k], 13 + k, sib)
    sib_has(xo)
    project(xo, False)

    @pl.loop(0, NE)
    def _(s):
        ps[s] = acc[pl.ds(pl.multiple_of(s * CAP, CAP), CAP), :].astype(BF)

        @pl.when(s != e)
        def _():
            rc(ps.at[s], pr.at[e], s_e.at[s], r_e.at[e], (s, r)).start()

        @pl.when(s == e)
        def _():
            pr[e] = ps[s]

    for k in range(2, 6):
        got(xr.at[k], r_x.at[k])

    def total(h, put):
        @pl.loop(0, 7)
        def _(i):
            rows = pl.ds(pl.multiple_of(i * 32, 32), 32)
            put(
                rows,
                part[rid(x, h, c), rows, :].astype(F32)
                + xr[2 + h, rows, :].astype(F32)
                + xr[5 - h, rows, :].astype(F32),
            )

    def put_part(rows, v):
        part[rid(x, 1 - yh, c), rows, :] = v.astype(BF)

    def put_g(rows, v):
        g[rows, :] = v

    total(1 - yh, put_part)
    ysend = rc(part.at[rid(x, 1 - yh, c)], yr, s_y.at[0], r_y.at[0], yp)
    ysend.start()
    total(yh, put_g)

    @pl.loop(1, NE)
    def _(d):
        s = (e + d) % NE
        got(b2r.at[s], r_b2.at[s])

    for i in range(NE):
        out = m1n if i < 4 else m2n
        a, b = (i // 2) % 2, i % 2
        out[112 * a : 112 * a + 112, 640 * b : 640 * b + 640] = b2r[i]

    @pl.loop(1, NE)
    def _(d):
        s = (e + d) % NE
        got(pr.at[s], r_e.at[s])

    @pl.loop(0, FW // TILE)
    def _(n):
        cols = pl.ds(pl.multiple_of(n * TILE, TILE), TILE)
        for k, ref in ((0, g0), (1, g1)):
            v = lax.dot_general(
                ref[...], pr[:, :, cols].reshape(ROWS, TILE), (((0,), (0,)), ((), ())), preferred_element_type=F32
            )
            act[:, pl.ds(pl.multiple_of(k * FW + n * TILE, TILE), TILE)] = v.astype(BF)

    ysend.wait_recv()

    @pl.loop(0, 7)
    def _(i):
        rows = pl.ds(pl.multiple_of(i * 32, 32), 32)
        g[rows, :] += yr[rows, :].astype(F32)

    ysend.wait_send()
    for k in range(15):
        gone(wfull.at[0], s_ag.at[k])

    @pl.loop(0, 7)
    def _(i):
        @pl.when(i != e)
        def _():
            gone(w1.at[0], s_w1.at[i])

    @pl.loop(0, NE)
    def _(s):
        gone(sibr.at[0], s_sb.at[s])

    @pl.loop(0, 6)
    def _(s):
        gone(xr.at[0], s_x.at[s])

    @pl.loop(1, NE)
    def _(d):
        s = (e + d) % NE

        @pl.when(e < 7)
        def _():
            gone(w2s.at[0], s_w2.at[s])

        gone(b1s.at[0], s_b1.at[s])
        gone(b2s.at[0], s_b2.at[s])
        gone(cp.at[0], s_c.at[s])
        gone(ps.at[0], s_e.at[s])
        for q in range(4):
            gone(tp.at[0, 0], s_t.at[q, s])


def send_chunk(q, e, r, tok, g0, g1, tp, tr, s_t, r_t, spread):
    cols = pl.ds(pl.multiple_of(q * CHUNK, 128), CHUNK)
    v = jnp.dot(g0[...] + g1[...], tok[:, cols], preferred_element_type=F32)
    tp[q] = v.astype(BF).reshape(NE, CAP, CHUNK)
    spread(lambda s: tp.at[q, s], lambda s: tr.at[q, s], lambda s: s_t.at[q, s], lambda s: r_t.at[q, s])
    tr[q, e] = tp[q, e]


def body(tokens, routes, cotangent, weights, first_moment, second_moment, pairing):
    dma = pltpu.SemaphoreType.DMA
    vmem = pl.BlockSpec(memory_space=pltpu.VMEM)
    hbm = pl.BlockSpec(memory_space=pl.ANY)
    act, wn, m1n, m2n, g = pl.pallas_call(
        kernel,
        out_shape=(
            jax.ShapeDtypeStruct((TOK, 2 * FW), BF),
            jax.ShapeDtypeStruct((SHARD, FW), BF),
            jax.ShapeDtypeStruct((SHARD, FW), BF),
            jax.ShapeDtypeStruct((SHARD, FW), BF),
            jax.ShapeDtypeStruct((SHARD, FW), F32),
        ),
        in_specs=[pl.BlockSpec(memory_space=pltpu.SMEM), vmem, vmem, vmem, vmem, hbm, hbm],
        out_specs=(vmem,) * 5,
        scratch_shapes=[
            pltpu.VMEM((NE, 32, FW), BF),
            pltpu.VMEM((NE, 32, FW), BF),
            pltpu.VMEM((16, SHARD, FW), BF),
            pltpu.VMEM((NE, 112, 640), BF),
            pltpu.VMEM((NE, 112, 640), BF),
            pltpu.VMEM((NE, 112, 640), BF),
            pltpu.VMEM((NE, 112, 640), BF),
            pltpu.VMEM((4, NE, CAP, CHUNK), BF),
            pltpu.VMEM((4, NE, CAP, CHUNK), BF),
            pltpu.VMEM((NE, CAP, FW), BF),
            pltpu.VMEM((NE, CAP, FW), BF),
            pltpu.VMEM((ROWS, FW), F32),
            pltpu.VMEM((NE, CAP, FW), BF),
            pltpu.VMEM((NE, CAP, FW), BF),
            pltpu.VMEM((16, SHARD, FW), BF),
            pltpu.VMEM((NE, SHARD, FW), BF),
            pltpu.VMEM((6, SHARD, FW), BF),
            pltpu.VMEM((SHARD, FW), BF),
            pltpu.VMEM((ROWS, TOK), BF),
            pltpu.VMEM((ROWS, TOK), BF),
            dma((2,)),
            dma((NE,)), dma((NE,)), dma((NE,)), dma((NE,)),
            dma((NE,)), dma((NE,)), dma((NE,)), dma((NE,)),
            dma((4, NE)), dma((4, NE)),
            dma((NE,)), dma((NE,)), dma((NE,)), dma((NE,)),
            dma((15,)), dma((16,)),
            dma((NE,)), dma((NE,)),
            dma((6,)), dma((6,)),
            dma((1,)), dma((1,)),
        ],
        compiler_params=pltpu.CompilerParams(
            collective_id=0, has_side_effects=True, vmem_limit_bytes=63 * 1024 * 1024
        ),
    )(
        pairing,
        routes.T,
        tokens,
        cotangent.reshape(TOK, 2 * FW),
        weights.reshape(SHARD, FW),
        first_moment.reshape(SHARD, FW),
        second_moment.reshape(SHARD, FW),
    )
    new_first = BETA_ONE * m1n.astype(F32) + (1.0 - BETA_ONE) * g
    new_second = BETA_TWO * m2n.astype(F32) + (1.0 - BETA_TWO) * g * g
    update = new_first / (jnp.sqrt(new_second) + EPSILON)
    shape = first_moment.shape
    return (
        act.reshape(TOK, 2, FW),
        wn.reshape(weights.shape),
        new_first.reshape(shape),
        new_second.reshape(shape),
        update.reshape(shape),
    )


def solution(mesh):
    in_specs = (
        P(("expert", "replica"), None),
        P(("expert", "replica"), None),
        P(("expert", "replica"), None, None),
        P("expert", "replica", None),
        P("expert", "replica", None),
        P("expert", "replica", None),
        P(),
    )
    out_specs = (
        P(("expert", "replica"), None, None),
        P("expert", "replica", None),
        P("expert", "replica", None),
        P("expert", "replica", None),
        P("expert", "replica", None),
    )
    return jax.shard_map(body, mesh=mesh, in_specs=in_specs, out_specs=out_specs, check_vma=False)
```

```python
import jax
import jax.numpy as jnp
from jax import lax
from jax.experimental import pallas as pl
from jax.experimental.pallas import tpu as pltpu
from jax.sharding import PartitionSpec as P

BETA_ONE = 0.8
BETA_TWO = 0.9
EPSILON = 1e-08
MESH = pl.DeviceIdType.MESH
BF = jnp.bfloat16
F32 = jnp.float32

D, FW, TOK, CAP, NE, SHARD, CHUNK = 3584, 1280, 128, 64, 8, 224, 896
ROWS = NE * CAP
TILE = 256
WIDE = 640
HALF = 112


def kernel(
    pair, rt, tok, cot, w, m1, m2,
    act, wn, m1n, m2n, g,
    w1, w2s, wfull, b1s, b1r, b2s, b2r, tp, tr, cp, cr, acc, ps, pr, part, sibr, xr, yr, g0, g1,
    rnb, tnb, cnb, near, far_,
    s_m, s_w1, r_w1, s_w2, r_w2, s_b1, r_b1, s_b2, r_b2, s_t, r_t, s_c, r_c, s_e, r_e,
    s_ag, r_ag, s_sb, r_sb, s_x, r_x, s_y, r_y, s_nb, r_nb,
):
    e = lax.axis_index("expert")
    r = lax.axis_index("replica")
    x = r // 4
    yh = (r // 2) % 2
    c = r % 2

    def rid(x_, yh_, c_):
        return x_ * 4 + yh_ * 2 + c_

    xp, xm, xo = (x + 1) % 4, (x + 3) % 4, (x + 2) % 4
    z, yl = e // 2, e % 2
    ne = e + 1 - 2 * yl
    nb = (ne, r)
    order = (xo, xp, xm, x)
    sib = (e, rid(x, yh, 1 - c))
    yp = (e, rid(x, 1 - yh, c))
    px = (e, rid(xp, yh, c))
    mx = (e, rid(xm, yh, c))

    def rc(src, dst, ss, rs, dev):
        return pltpu.make_async_remote_copy(
            src_ref=src, dst_ref=dst, send_sem=ss, recv_sem=rs, device_id=dev, device_id_type=MESH
        )

    def got(ref, sem):
        rc(ref, ref, sem, sem, sib).wait_recv()

    def gone(ref, sem):
        rc(ref, ref, sem, sem, sib).wait_send()

    loads = [
        pltpu.make_async_copy(m1, acc.at[pl.ds(0, SHARD)], s_m.at[0]),
        pltpu.make_async_copy(m2, acc.at[pl.ds(SHARD, SHARD)], s_m.at[1]),
    ]
    for load in loads:
        load.start()

    barrier = pltpu.get_barrier_semaphore()

    @pl.loop(1, NE)
    def _(d):
        pl.semaphore_signal(barrier, inc=1, device_id=((e + d) % NE, r), device_id_type=MESH)

    for dev in (sib, yp, px, mx):
        pl.semaphore_signal(barrier, inc=1, device_id=dev, device_id_type=MESH)
    pl.semaphore_wait(barrier, NE - 1 + 4)

    def raw(k):
        cols = pl.ds(pl.multiple_of(order[k] * CHUNK, 128), CHUNK)
        return rc(tok.at[:, cols], tnb.at[k], s_nb.at[k], r_nb.at[k], nb)

    raw_routes = rc(rt, rnb, s_nb.at[4], r_nb.at[4], nb)
    raw_cot = rc(cot, cnb, s_nb.at[5], r_nb.at[5], nb)
    raw_routes.start()

    @pl.loop(0, 7)
    def _(i):
        rows = pl.ds(pl.multiple_of(i * 32, 32), 32)

        @pl.when(i != e)
        def _():
            rc(w.at[rows], w1.at[e], s_w1.at[i], r_w1.at[e], (i, r)).start()

        @pl.when(i == e)
        def _():
            w1[e] = w[rows, :]

    raw(0).start()

    places = lax.broadcasted_iota(jnp.int32, (NE, TOK), 0)
    earlier = jnp.where(
        lax.broadcasted_iota(jnp.int32, (TOK, TOK), 0) < lax.broadcasted_iota(jnp.int32, (TOK, TOK), 1), 1.0, 0.0
    ).astype(BF)

    def placed(ref):
        owners = []
        for k in range(2):
            row = ref[k : k + 1, :]
            own = jnp.zeros_like(row)
            for s in range(NE):
                own = own + jnp.where(row == s, pair[s], 0)
            owners.append(own)
        named = [(places == own) for own in owners]
        mask = jnp.where(named[0] | named[1], 1.0, 0.0).astype(BF)
        rank = jnp.dot(mask, earlier, preferred_element_type=F32)
        ranks = [jnp.sum(jnp.where(one, rank, 0.0), axis=0, keepdims=True) for one in named]
        return owners, ranks

    def one_hot(slot, ref, rows):
        slots = lax.broadcasted_iota(jnp.int32, (rows, TOK), 0).astype(F32)
        ref[...] = jnp.where(slots == slot, 1.0, 0.0).astype(BF)

    def along_z(owners, ranks, ref):
        for k in range(2):
            slot = (owners[k] >> 1).astype(F32) * CAP + ranks[k]
            one_hot(jnp.where((owners[k] & 1) == yl, slot, -1.0), ref.at[k], NE * CAP // 2)

    owners, ranks = placed(rt)
    along_z(owners, ranks, near)

    def to_z(src, dst, ss, rs):
        @pl.loop(1, 4)
        def _(d):
            t = (z + d) % 4
            rc(src(t), dst, ss(t), rs, (t * 2 + yl, r)).start()

    def send_cot(half):
        hot, src, owner = ((near, cot, e), (far_, cnb, ne))[half]

        @pl.loop(0, FW // TILE)
        def _(n):
            cols = pl.ds(pl.multiple_of(n * TILE, TILE), TILE)
            a = jnp.dot(hot[0], src[:, 0, cols], preferred_element_type=F32)
            b = jnp.dot(hot[1], src[:, 1, cols], preferred_element_type=F32)
            cp[half, :, :, cols] = (a + b).astype(BF).reshape(4, CAP, TILE)

        to_z(lambda t: cp.at[half, t], cr.at[owner], lambda t: s_c.at[half, t], r_c.at[owner])
        cr[owner] = cp[half, z]

    def send_tok(half, k):
        hot, owner = ((near, e), (far_, ne))[half]
        q = order[k]
        src = tok[:, pl.ds(pl.multiple_of(q * CHUNK, 128), CHUNK)] if half == 0 else tnb[k]
        v = jnp.dot(hot[0] + hot[1], src, preferred_element_type=F32)
        tp[k, half] = v.astype(BF).reshape(4, CAP, CHUNK)
        to_z(lambda t: tp.at[k, half, t], tr.at[q, owner], lambda t: s_t.at[k, half, t], r_t.at[k, owner])
        tr[q, owner] = tp[k, half, z]

    send_cot(0)

    @pl.when(e < 7)
    def _():
        @pl.loop(0, NE)
        def _(s):
            @pl.when(s != e)
            def _():
                got(w1.at[s], r_w1.at[s])

        rows = pl.ds(pl.multiple_of(e * 32, 32), 32)

        @pl.loop(0, NE)
        def _(s):
            v = w1[pair[s]]
            w2s[s] = v

            @pl.when(s != e)
            def _():
                rc(w2s.at[s], wfull.at[r, rows], s_w2.at[s], r_w2.at[e], (s, r)).start()

            @pl.when(s == e)
            def _():
                wfull[r, rows, :] = v

    send_tok(0, 0)
    send_tok(0, 1)
    raw_routes.wait_recv()
    along_z(*placed(rnb), far_)
    for k in range(2):
        one_hot(owners[k].astype(F32) * CAP + ranks[k], (g0, g1)[k], ROWS)

    @pl.loop(0, 7)
    def _(i):
        @pl.when(i != e)
        def _():
            got(wfull.at[r, pl.ds(pl.multiple_of(i * 32, 32), 32)], r_w2.at[i])

    def ag(shard, k, dev):
        rc(wfull.at[shard], wfull.at[shard], s_ag.at[k], r_ag.at[shard], dev).start()

    ag(r, 0, yp)
    ag(r, 1, px)
    ag(r, 2, mx)
    ag(r, 3, sib)

    raw_cot.start()
    for k in range(1, 4):
        raw(k).start()
    send_tok(0, 2)
    send_tok(0, 3)
    raw(0).wait_recv()
    send_tok(1, 0)
    wn[...] = wfull[r]

    def from_x(h, k):
        low, high = rid(xm, h, c), rid(xp, h, c)
        got(wfull.at[low], r_ag.at[low])
        ag(low, k, sib)
        got(wfull.at[high], r_ag.at[high])
        ag(high, k + 1, sib)
        ag(rid((x + 3 + 2 * h) % 4, h, c), k + 2, (e, rid((x + 1 + 2 * h) % 4, yh, c)))

    partner = rid(x, 1 - yh, c)
    got(wfull.at[partner], r_ag.at[partner])
    ag(partner, 4, px)
    ag(partner, 5, mx)
    ag(partner, 6, sib)
    from_x(yh, 7)

    def other_z(take):
        @pl.loop(1, 4)
        def _(d):
            t = (z + d) % 4
            take(t * 2 + yl)
            take(t * 2 + 1 - yl)

    def wgrad(k):
        q = order[k]
        other_z(lambda s: got(tr.at[q, s], r_t.at[k, s]))

        @pl.loop(0, FW // WIDE)
        def _(n):
            cols = pl.ds(pl.multiple_of(n * WIDE, WIDE), WIDE)
            v = lax.dot_general(
                tr[q].reshape(ROWS, CHUNK), cr[:, :, cols].reshape(ROWS, WIDE), (((0,), (0,)), ((), ())),
                preferred_element_type=F32,
            )
            part[pl.ds(q * 4, 4), :, cols] = v.astype(BF).reshape(4, SHARD, WIDE)

    def add(shard, other, half):
        @pl.loop(0, 7)
        def _(i):
            rows = pl.ds(pl.multiple_of(half * HALF + i * 16, 16), 16)
            part[shard, rows, :] = (part[shard, rows, :].astype(F32) + other[rows, :].astype(F32)).astype(BF)

    def to_sib(k):
        for h in range(2):
            rc(
                part.at[rid(order[k], h, 1 - c)], sibr.at[2 * k + h], s_sb.at[2 * k + h], r_sb.at[2 * k + h], sib
            ).start()

    def xs(h, k, slot, half, dev):
        rows = pl.ds(half * HALF, HALF)
        rc(
            part.at[rid(order[k], h, c), rows], xr.at[slot, rows], s_x.at[slot, half], r_x.at[slot, half], dev
        ).start()

    def with_sib(k, h, slot=None, dev=None):
        got(sibr.at[2 * k + h], r_sb.at[2 * k + h])
        for half in range(2):
            add(rid(order[k], h, c), sibr.at[2 * k + h], half)
            if dev is not None:
                xs(h, k, slot, half, dev)

    def with_x(k, h, came, slot, dev):
        for half in range(2):
            got(xr.at[came, pl.ds(half * HALF, HALF)], r_x.at[came, half])
            add(rid(order[k], h, c), xr.at[came], half)
            xs(h, k, slot, half, dev)

    def project(q, first):
        @pl.loop(0, FW // WIDE)
        def _(n):
            cols = pl.ds(pl.multiple_of(n * WIDE, WIDE), WIDE)
            v = jnp.dot(
                tr[q].reshape(ROWS, CHUNK), wfull[pl.ds(q * 4, 4), :, cols].reshape(CHUNK, WIDE),
                preferred_element_type=F32,
            )
            if first:
                acc[:, cols] = v
            else:
                acc[:, cols] += v

    def sib_has(q):
        for h in range(2):
            shard = rid(q, h, 1 - c)
            got(wfull.at[shard], r_ag.at[shard])


    raw_cot.wait_recv()
    send_cot(1)
    raw(1).wait_recv()
    send_tok(1, 1)
    from_x(1 - yh, 10)

    other_z(lambda s: got(cr.at[s], r_c.at[s]))
    wgrad(0)
    to_sib(0)
    raw(2).wait_recv()
    send_tok(1, 2)
    with_sib(0, 0, 0, px)
    with_sib(0, 1, 1, mx)
    raw(3).wait_recv()
    send_tok(1, 3)

    for load in loads:
        load.wait()

    @pl.loop(0, NE)
    def _(p):
        rows = pl.ds(pl.multiple_of((p // 4) * SHARD + ((p // 2) % 2) * 112, 8), 112)
        cols = pl.ds(pl.multiple_of((p % 2) * 640, 128), 640)
        b1s[p] = acc[rows, cols].astype(BF)

        @pl.when(p != e)
        def _():
            rc(b1s.at[p], b1r.at[e], s_b1.at[p], r_b1.at[e], (p, r)).start()

        @pl.when(p == e)
        def _():
            b1r[e] = b1s[p]

    wgrad(1)
    to_sib(1)
    far = (rid(xo, yh, c), rid(xo, 1 - yh, c))
    for k in range(2):
        got(wfull.at[far[k]], r_ag.at[far[k]])
        ag(far[k], 13 + k, sib)
    with_sib(1, 1, 3, px)
    with_sib(1, 0)
    wgrad(2)
    to_sib(2)
    sib_has(xo)
    project(xo, True)
    with_sib(2, 0, 5, mx)
    with_sib(2, 1)
    wgrad(3)
    to_sib(3)
    sib_has(xp)
    project(xp, False)
    sib_has(xm)
    project(xm, False)
    sib_has(x)
    project(x, False)

    @pl.loop(0, NE)
    def _(s):
        ps[s] = acc[pl.ds(pl.multiple_of(s * CAP, CAP), CAP), :].astype(BF)

        @pl.when(s != e)
        def _():
            rc(ps.at[s], pr.at[e], s_e.at[s], r_e.at[e], (s, r)).start()

        @pl.when(s == e)
        def _():
            pr[e] = ps[s]

    with_x(1, 0, 0, 2, px)
    with_x(2, 1, 1, 4, mx)
    with_sib(3, 0)
    with_sib(3, 1)

    @pl.loop(1, NE)
    def _(d):
        s = (e + d) % NE
        got(b1r.at[s], r_b1.at[s])

    @pl.loop(0, NE)
    def _(s):
        v = b1r[pair[s]]
        b2s[s] = v

        @pl.when(s != e)
        def _():
            rc(b2s.at[s], b2r.at[e], s_b2.at[s], r_b2.at[e], (s, r)).start()

        @pl.when(s == e)
        def _():
            b2r[e] = v

    def total(h, half, put):
        @pl.loop(0, 7)
        def _(i):
            rows = pl.ds(pl.multiple_of(half * HALF + i * 16, 16), 16)
            put(
                rows,
                part[rid(x, h, c), rows, :].astype(F32)
                + xr[2 + h, rows, :].astype(F32)
                + xr[5 - h, rows, :].astype(F32),
            )

    def put_part(rows, v):
        part[partner, rows, :] = v.astype(BF)

    def put_g(rows, v):
        g[rows, :] = v

    def ysend(half):
        rows = pl.ds(half * HALF, HALF)
        return rc(part.at[partner, rows], yr.at[rows], s_y.at[half], r_y.at[half], yp)

    for half in range(2):
        for k in range(2, 6):
            got(xr.at[k, pl.ds(half * HALF, HALF)], r_x.at[k, half])
        total(1 - yh, half, put_part)
        ysend(half).start()
        total(yh, half, put_g)

    @pl.loop(1, NE)
    def _(d):
        s = (e + d) % NE
        got(b2r.at[s], r_b2.at[s])

    for i in range(NE):
        out = m1n if i < 4 else m2n
        a, b = (i // 2) % 2, i % 2
        out[112 * a : 112 * a + 112, 640 * b : 640 * b + 640] = b2r[i]

    @pl.loop(1, NE)
    def _(d):
        s = (e + d) % NE
        got(pr.at[s], r_e.at[s])

    @pl.loop(0, FW // TILE)
    def _(n):
        cols = pl.ds(pl.multiple_of(n * TILE, TILE), TILE)
        for k, ref in ((0, g0), (1, g1)):
            v = lax.dot_general(
                ref[...], pr[:, :, cols].reshape(ROWS, TILE), (((0,), (0,)), ((), ())), preferred_element_type=F32
            )
            act[:, k, cols] = v.astype(BF)

    for half in range(2):
        ysend(half).wait_recv()

        @pl.loop(0, 7)
        def _(i):
            rows = pl.ds(pl.multiple_of(half * HALF + i * 16, 16), 16)
            g[rows, :] += yr[rows, :].astype(F32)

    for half in range(2):
        ysend(half).wait_send()
    for k in range(15):
        gone(wfull.at[0], s_ag.at[k])

    @pl.loop(0, 7)
    def _(i):
        @pl.when(i != e)
        def _():
            gone(w1.at[0], s_w1.at[i])

    @pl.loop(0, NE)
    def _(s):
        gone(sibr.at[0], s_sb.at[s])

    @pl.loop(0, 6)
    def _(s):
        for half in range(2):
            gone(xr.at[0, pl.ds(0, HALF)], s_x.at[s, half])

    @pl.loop(1, NE)
    def _(d):
        s = (e + d) % NE

        @pl.when(e < 7)
        def _():
            gone(w2s.at[0], s_w2.at[s])

        gone(b1s.at[0], s_b1.at[s])
        gone(b2s.at[0], s_b2.at[s])
        gone(ps.at[0], s_e.at[s])

    @pl.loop(1, 4)
    def _(d):
        t = (z + d) % 4
        for half in range(2):
            gone(cp.at[0, 0], s_c.at[half, t])
            for k in range(4):
                gone(tp.at[0, 0, 0], s_t.at[k, half, t])

    raw_routes.wait_send()
    raw_cot.wait_send()
    for k in range(4):
        raw(k).wait_send()


def body(tokens, routes, cotangent, weights, first_moment, second_moment, pairing):
    dma = pltpu.SemaphoreType.DMA
    vmem = pl.BlockSpec(memory_space=pltpu.VMEM)
    hbm = pl.BlockSpec(memory_space=pl.ANY)
    act, wn, m1n, m2n, g = pl.pallas_call(
        kernel,
        out_shape=(
            jax.ShapeDtypeStruct((TOK, 2, FW), BF),
            jax.ShapeDtypeStruct((SHARD, FW), BF),
            jax.ShapeDtypeStruct((SHARD, FW), BF),
            jax.ShapeDtypeStruct((SHARD, FW), BF),
            jax.ShapeDtypeStruct((SHARD, FW), F32),
        ),
        in_specs=[pl.BlockSpec(memory_space=pltpu.SMEM), vmem, vmem, vmem, vmem, hbm, hbm],
        out_specs=(vmem,) * 5,
        scratch_shapes=[
            pltpu.VMEM((NE, 32, FW), BF),
            pltpu.VMEM((NE, 32, FW), BF),
            pltpu.VMEM((16, SHARD, FW), BF),
            pltpu.VMEM((NE, 112, 640), BF),
            pltpu.VMEM((NE, 112, 640), BF),
            pltpu.VMEM((NE, 112, 640), BF),
            pltpu.VMEM((NE, 112, 640), BF),
            pltpu.VMEM((4, 2, 4, CAP, CHUNK), BF),
            pltpu.VMEM((4, NE, CAP, CHUNK), BF),
            pltpu.VMEM((2, 4, CAP, FW), BF),
            pltpu.VMEM((NE, CAP, FW), BF),
            pltpu.VMEM((ROWS, FW), F32),
            pltpu.VMEM((NE, CAP, FW), BF),
            pltpu.VMEM((NE, CAP, FW), BF),
            pltpu.VMEM((16, SHARD, FW), BF),
            pltpu.VMEM((NE, SHARD, FW), BF),
            pltpu.VMEM((6, SHARD, FW), BF),
            pltpu.VMEM((SHARD, FW), BF),
            pltpu.VMEM((ROWS, TOK), BF),
            pltpu.VMEM((ROWS, TOK), BF),
            pltpu.VMEM((2, TOK), jnp.int32),
            pltpu.VMEM((4, TOK, CHUNK), BF),
            pltpu.VMEM((TOK, 2, FW), BF),
            pltpu.VMEM((2, ROWS // 2, TOK), BF),
            pltpu.VMEM((2, ROWS // 2, TOK), BF),
            dma((2,)),
            dma((NE,)), dma((NE,)), dma((NE,)), dma((NE,)),
            dma((NE,)), dma((NE,)), dma((NE,)), dma((NE,)),
            dma((4, 2, 4)), dma((4, NE)),
            dma((2, 4)), dma((NE,)), dma((NE,)), dma((NE,)),
            dma((15,)), dma((16,)),
            dma((NE,)), dma((NE,)),
            dma((6, 2)), dma((6, 2)),
            dma((2,)), dma((2,)),
            dma((6,)), dma((6,)),
        ],
        compiler_params=pltpu.CompilerParams(
            collective_id=0, has_side_effects=True, vmem_limit_bytes=63 * 1024 * 1024
        ),
    )(
        pairing,
        routes.T,
        tokens,
        cotangent,
        weights.reshape(SHARD, FW),
        first_moment.reshape(SHARD, FW),
        second_moment.reshape(SHARD, FW),
    )
    new_first = BETA_ONE * m1n.astype(F32) + (1.0 - BETA_ONE) * g
    new_second = BETA_TWO * m2n.astype(F32) + (1.0 - BETA_TWO) * g * g
    update = new_first / (jnp.sqrt(new_second) + EPSILON)
    shape = first_moment.shape
    return (
        act,
        wn.reshape(weights.shape),
        new_first.reshape(shape),
        new_second.reshape(shape),
        update.reshape(shape),
    )


def solution(mesh):
    in_specs = (
        P(("expert", "replica"), None),
        P(("expert", "replica"), None),
        P(("expert", "replica"), None, None),
        P("expert", "replica", None),
        P("expert", "replica", None),
        P("expert", "replica", None),
        P(),
    )
    out_specs = (
        P(("expert", "replica"), None, None),
        P("expert", "replica", None),
        P("expert", "replica", None),
        P("expert", "replica", None),
        P("expert", "replica", None),
    )
    return jax.shard_map(body, mesh=mesh, in_specs=in_specs, out_specs=out_specs, check_vma=False)
```

```python
import jax
import jax.numpy as jnp
from jax import lax
from jax.experimental import pallas as pl
from jax.experimental.pallas import tpu as pltpu
from jax.sharding import PartitionSpec as P

BETA_ONE = 0.8
BETA_TWO = 0.9
EPSILON = 1e-08
MESH = pl.DeviceIdType.MESH
BF = jnp.bfloat16
F32 = jnp.float32

D, FW, TOK, CAP, NE, SHARD, CHUNK = 3584, 1280, 128, 64, 8, 224, 896
ROWS = NE * CAP
TILE = 256
WIDE = 640
HALF = 112


def kernel(
    pair, rt, tok, cot, w, m1, m2,
    act, wn, m1n, m2n, g,
    w1, w2s, wfull, b1s, b1r, b2s, b2r, tp, tr, cp, cr, acc, ps, pr, part, sibr, xr, yr, g0, g1,
    rnb, tnb, cnb, near, far_,
    s_m, s_w1, r_w1, s_w2, r_w2, s_b1, r_b1, s_b2, r_b2, s_t, r_t, s_c, r_c, s_e, r_e,
    s_ag, r_ag, s_sb, r_sb, s_x, r_x, s_y, r_y, s_nb, r_nb,
):
    e = lax.axis_index("expert")
    r = lax.axis_index("replica")
    x = r // 4
    yh = (r // 2) % 2
    c = r % 2

    def rid(x_, yh_, c_):
        return x_ * 4 + yh_ * 2 + c_

    xp, xm, xo = (x + 1) % 4, (x + 3) % 4, (x + 2) % 4
    z, yl = e // 2, e % 2
    ne = e + 1 - 2 * yl
    nb = (ne, r)
    order = (xo, xp, xm, x)
    sib = (e, rid(x, yh, 1 - c))
    yp = (e, rid(x, 1 - yh, c))
    px = (e, rid(xp, yh, c))
    mx = (e, rid(xm, yh, c))

    def rc(src, dst, ss, rs, dev):
        return pltpu.make_async_remote_copy(
            src_ref=src, dst_ref=dst, send_sem=ss, recv_sem=rs, device_id=dev, device_id_type=MESH
        )

    def got(ref, sem):
        rc(ref, ref, sem, sem, sib).wait_recv()

    def gone(ref, sem):
        rc(ref, ref, sem, sem, sib).wait_send()

    loads = [
        pltpu.make_async_copy(m1, acc.at[pl.ds(0, SHARD)], s_m.at[0]),
        pltpu.make_async_copy(m2, acc.at[pl.ds(SHARD, SHARD)], s_m.at[1]),
    ]
    for load in loads:
        load.start()

    barrier = pltpu.get_barrier_semaphore()

    @pl.loop(1, NE)
    def _(d):
        pl.semaphore_signal(barrier, inc=1, device_id=((e + d) % NE, r), device_id_type=MESH)

    for dev in (sib, yp, px, mx):
        pl.semaphore_signal(barrier, inc=1, device_id=dev, device_id_type=MESH)
    pl.semaphore_wait(barrier, NE - 1 + 4)

    def raw(k):
        cols = pl.ds(pl.multiple_of(order[k] * CHUNK, 128), CHUNK)
        return rc(tok.at[:, cols], tnb.at[k], s_nb.at[k], r_nb.at[k], nb)

    raw_routes = rc(rt, rnb, s_nb.at[4], r_nb.at[4], nb)
    raw_cot = rc(cot, cnb, s_nb.at[5], r_nb.at[5], nb)
    raw_routes.start()

    @pl.loop(1, NE)
    def _(d):
        i = (e + d) % NE

        @pl.when(i < 7)
        def _():
            rows = pl.ds(pl.multiple_of(i * 32, 32), 32)
            rc(w.at[rows], w1.at[e], s_w1.at[i], r_w1.at[e], (i, r)).start()

    @pl.when(e < 7)
    def _():
        w1[e] = w[pl.ds(pl.multiple_of(e * 32, 32), 32), :]

    raw(0).start()

    places = lax.broadcasted_iota(jnp.int32, (NE, TOK), 0)
    earlier = jnp.where(
        lax.broadcasted_iota(jnp.int32, (TOK, TOK), 0) < lax.broadcasted_iota(jnp.int32, (TOK, TOK), 1), 1.0, 0.0
    ).astype(BF)

    def placed(ref):
        owners = []
        for k in range(2):
            row = ref[k : k + 1, :]
            own = jnp.zeros_like(row)
            for s in range(NE):
                own = own + jnp.where(row == s, pair[s], 0)
            owners.append(own)
        named = [(places == own) for own in owners]
        mask = jnp.where(named[0] | named[1], 1.0, 0.0).astype(BF)
        rank = jnp.dot(mask, earlier, preferred_element_type=F32)
        ranks = [jnp.sum(jnp.where(one, rank, 0.0), axis=0, keepdims=True) for one in named]
        return owners, ranks

    def one_hot(slot, ref, rows):
        slots = lax.broadcasted_iota(jnp.int32, (rows, TOK), 0).astype(F32)
        ref[...] = jnp.where(slots == slot, 1.0, 0.0).astype(BF)

    def along_z(owners, ranks, ref):
        for k in range(2):
            slot = (owners[k] >> 1).astype(F32) * CAP + ranks[k]
            one_hot(jnp.where((owners[k] & 1) == yl, slot, -1.0), ref.at[k], NE * CAP // 2)

    owners, ranks = placed(rt)
    along_z(owners, ranks, near)

    def to_z(src, dst, ss, rs):
        @pl.loop(1, 4)
        def _(d):
            t = (z + d) % 4
            rc(src(t), dst, ss(t), rs, (t * 2 + yl, r)).start()

    def send_cot(half):
        hot, src, owner = ((near, cot, e), (far_, cnb, ne))[half]

        @pl.loop(0, FW // TILE)
        def _(n):
            cols = pl.ds(pl.multiple_of(n * TILE, TILE), TILE)
            a = jnp.dot(hot[0], src[:, 0, cols], preferred_element_type=F32)
            b = jnp.dot(hot[1], src[:, 1, cols], preferred_element_type=F32)
            cp[half, :, :, cols] = (a + b).astype(BF).reshape(4, CAP, TILE)

        to_z(lambda t: cp.at[half, t], cr.at[owner], lambda t: s_c.at[half, t], r_c.at[owner])
        cr[owner] = cp[half, z]

    def send_tok(half, k):
        hot, owner = ((near, e), (far_, ne))[half]
        q = order[k]
        src = tok[:, pl.ds(pl.multiple_of(q * CHUNK, 128), CHUNK)] if half == 0 else tnb[k]
        v = jnp.dot(hot[0] + hot[1], src, preferred_element_type=F32)
        tp[k, half] = v.astype(BF).reshape(4, CAP, CHUNK)
        to_z(lambda t: tp.at[k, half, t], tr.at[q, owner], lambda t: s_t.at[k, half, t], r_t.at[k, owner])
        tr[q, owner] = tp[k, half, z]

    send_cot(0)

    @pl.when(e < 7)
    def _():
        @pl.loop(0, NE)
        def _(s):
            @pl.when(s != e)
            def _():
                got(w1.at[s], r_w1.at[s])

        rows = pl.ds(pl.multiple_of(e * 32, 32), 32)

        @pl.loop(1, NE + 1)
        def _(d):
            s = (e + d) % NE
            v = w1[pair[s]]
            w2s[s] = v

            @pl.when(s != e)
            def _():
                rc(w2s.at[s], wfull.at[r, rows], s_w2.at[s], r_w2.at[e], (s, r)).start()

            @pl.when(s == e)
            def _():
                wfull[r, rows, :] = v

    send_tok(0, 0)
    send_tok(0, 1)
    raw_routes.wait_recv()
    along_z(*placed(rnb), far_)
    for k in range(2):
        one_hot(owners[k].astype(F32) * CAP + ranks[k], (g0, g1)[k], ROWS)

    @pl.loop(0, 7)
    def _(i):
        @pl.when(i != e)
        def _():
            got(wfull.at[r, pl.ds(pl.multiple_of(i * 32, 32), 32)], r_w2.at[i])

    def ag(shard, k, dev):
        rc(wfull.at[shard], wfull.at[shard], s_ag.at[k], r_ag.at[shard], dev).start()

    ag(r, 0, yp)
    ag(r, 1, px)
    ag(r, 2, mx)
    ag(r, 3, sib)

    raw_cot.start()
    for k in range(1, 4):
        raw(k).start()
    send_tok(0, 2)
    send_tok(0, 3)
    raw(0).wait_recv()
    send_tok(1, 0)
    wn[...] = wfull[r]

    def from_x(h, k):
        low, high = rid(xm, h, c), rid(xp, h, c)
        got(wfull.at[low], r_ag.at[low])
        ag(low, k, sib)
        got(wfull.at[high], r_ag.at[high])
        ag(high, k + 1, sib)
        ag(rid((x + 3 + 2 * h) % 4, h, c), k + 2, (e, rid((x + 1 + 2 * h) % 4, yh, c)))

    partner = rid(x, 1 - yh, c)
    got(wfull.at[partner], r_ag.at[partner])
    ag(partner, 4, px)
    ag(partner, 5, mx)
    ag(partner, 6, sib)
    from_x(yh, 7)

    def other_z(take):
        @pl.loop(1, 4)
        def _(d):
            t = (z + d) % 4
            take(t * 2 + yl)
            take(t * 2 + 1 - yl)

    def wgrad(k):
        q = order[k]
        other_z(lambda s: got(tr.at[q, s], r_t.at[k, s]))

        @pl.loop(0, FW // WIDE)
        def _(n):
            cols = pl.ds(pl.multiple_of(n * WIDE, WIDE), WIDE)
            v = lax.dot_general(
                tr[q].reshape(ROWS, CHUNK), cr[:, :, cols].reshape(ROWS, WIDE), (((0,), (0,)), ((), ())),
                preferred_element_type=F32,
            )
            part[pl.ds(q * 4, 4), :, cols] = v.astype(BF).reshape(4, SHARD, WIDE)

    def add(shard, other, half):
        @pl.loop(0, 7)
        def _(i):
            rows = pl.ds(pl.multiple_of(half * HALF + i * 16, 16), 16)
            part[shard, rows, :] = (part[shard, rows, :].astype(F32) + other[rows, :].astype(F32)).astype(BF)

    def to_sib(k):
        for h in range(2):
            rc(
                part.at[rid(order[k], h, 1 - c)], sibr.at[2 * k + h], s_sb.at[2 * k + h], r_sb.at[2 * k + h], sib
            ).start()

    def xs(h, k, slot, half, dev):
        rows = pl.ds(half * HALF, HALF)
        rc(
            part.at[rid(order[k], h, c), rows], xr.at[slot, rows], s_x.at[slot, half], r_x.at[slot, half], dev
        ).start()

    def with_sib(k, h, slot=None, dev=None):
        got(sibr.at[2 * k + h], r_sb.at[2 * k + h])
        for half in range(2):
            add(rid(order[k], h, c), sibr.at[2 * k + h], half)
            if dev is not None:
                xs(h, k, slot, half, dev)

    def with_x(k, h, came, slot, dev):
        for half in range(2):
            got(xr.at[came, pl.ds(half * HALF, HALF)], r_x.at[came, half])
            add(rid(order[k], h, c), xr.at[came], half)
            xs(h, k, slot, half, dev)

    def project(q, first):
        @pl.loop(0, FW // WIDE)
        def _(n):
            cols = pl.ds(pl.multiple_of(n * WIDE, WIDE), WIDE)
            v = jnp.dot(
                tr[q].reshape(ROWS, CHUNK), wfull[pl.ds(q * 4, 4), :, cols].reshape(CHUNK, WIDE),
                preferred_element_type=F32,
            )
            if first:
                acc[:, cols] = v
            else:
                acc[:, cols] += v

    def sib_has(q):
        for h in range(2):
            shard = rid(q, h, 1 - c)
            got(wfull.at[shard], r_ag.at[shard])


    raw_cot.wait_recv()
    send_cot(1)
    from_x(1 - yh, 10)
    raw(1).wait_recv()
    send_tok(1, 1)

    other_z(lambda s: got(cr.at[s], r_c.at[s]))
    wgrad(0)
    to_sib(0)
    raw(2).wait_recv()
    send_tok(1, 2)
    with_sib(0, 0, 0, px)
    with_sib(0, 1, 1, mx)
    raw(3).wait_recv()
    send_tok(1, 3)

    for load in loads:
        load.wait()

    @pl.loop(1, NE + 1)
    def _(d):
        p = (e + d) % NE
        rows = pl.ds(pl.multiple_of((p // 4) * SHARD + ((p // 2) % 2) * 112, 8), 112)
        cols = pl.ds(pl.multiple_of((p % 2) * 640, 128), 640)
        b1s[p] = acc[rows, cols].astype(BF)

        @pl.when(p != e)
        def _():
            rc(b1s.at[p], b1r.at[e], s_b1.at[p], r_b1.at[e], (p, r)).start()

        @pl.when(p == e)
        def _():
            b1r[e] = b1s[p]

    wgrad(1)
    to_sib(1)
    far = (rid(xo, yh, c), rid(xo, 1 - yh, c))
    for k in range(2):
        got(wfull.at[far[k]], r_ag.at[far[k]])
        ag(far[k], 13 + k, sib)
    with_sib(1, 1, 3, px)
    with_sib(1, 0)
    sib_has(xp)
    project(xp, True)
    wgrad(2)
    to_sib(2)
    with_sib(2, 0, 5, mx)
    with_sib(2, 1)
    sib_has(xm)
    project(xm, False)
    sib_has(xo)
    project(xo, False)
    wgrad(3)
    to_sib(3)
    sib_has(x)
    project(x, False)

    @pl.loop(1, NE + 1)
    def _(d):
        s = (e + d) % NE
        ps[s] = acc[pl.ds(pl.multiple_of(s * CAP, CAP), CAP), :].astype(BF)

        @pl.when(s != e)
        def _():
            rc(ps.at[s], pr.at[e], s_e.at[s], r_e.at[e], (s, r)).start()

        @pl.when(s == e)
        def _():
            pr[e] = ps[s]

    with_x(1, 0, 0, 2, px)
    with_x(2, 1, 1, 4, mx)
    with_sib(3, 0)
    with_sib(3, 1)

    @pl.loop(1, NE)
    def _(d):
        s = (e + d) % NE
        got(b1r.at[s], r_b1.at[s])

    @pl.loop(1, NE + 1)
    def _(d):
        s = (e + d) % NE
        v = b1r[pair[s]]
        b2s[s] = v

        @pl.when(s != e)
        def _():
            rc(b2s.at[s], b2r.at[e], s_b2.at[s], r_b2.at[e], (s, r)).start()

        @pl.when(s == e)
        def _():
            b2r[e] = v

    def total(h, half, put):
        @pl.loop(0, 7)
        def _(i):
            rows = pl.ds(pl.multiple_of(half * HALF + i * 16, 16), 16)
            put(
                rows,
                part[rid(x, h, c), rows, :].astype(F32)
                + xr[2 + h, rows, :].astype(F32)
                + xr[5 - h, rows, :].astype(F32),
            )

    def put_part(rows, v):
        part[partner, rows, :] = v.astype(BF)

    def put_g(rows, v):
        g[rows, :] = v

    def ysend(half):
        rows = pl.ds(half * HALF, HALF)
        return rc(part.at[partner, rows], yr.at[rows], s_y.at[half], r_y.at[half], yp)

    for half in range(2):
        for k in range(2, 6):
            got(xr.at[k, pl.ds(half * HALF, HALF)], r_x.at[k, half])
        total(1 - yh, half, put_part)
        ysend(half).start()
        total(yh, half, put_g)

    @pl.loop(1, NE)
    def _(d):
        s = (e + d) % NE
        got(b2r.at[s], r_b2.at[s])

    for i in range(NE):
        out = m1n if i < 4 else m2n
        a, b = (i // 2) % 2, i % 2
        out[112 * a : 112 * a + 112, 640 * b : 640 * b + 640] = b2r[i]

    @pl.loop(1, NE)
    def _(d):
        s = (e + d) % NE
        got(pr.at[s], r_e.at[s])

    @pl.loop(0, FW // TILE)
    def _(n):
        cols = pl.ds(pl.multiple_of(n * TILE, TILE), TILE)
        for k, ref in ((0, g0), (1, g1)):
            v = lax.dot_general(
                ref[...], pr[:, :, cols].reshape(ROWS, TILE), (((0,), (0,)), ((), ())), preferred_element_type=F32
            )
            act[:, k, cols] = v.astype(BF)

    for half in range(2):
        ysend(half).wait_recv()

        @pl.loop(0, 7)
        def _(i):
            rows = pl.ds(pl.multiple_of(half * HALF + i * 16, 16), 16)
            g[rows, :] += yr[rows, :].astype(F32)

    for half in range(2):
        ysend(half).wait_send()
    for k in range(15):
        gone(wfull.at[0], s_ag.at[k])

    @pl.loop(0, 7)
    def _(i):
        @pl.when(i != e)
        def _():
            gone(w1.at[0], s_w1.at[i])

    @pl.loop(0, NE)
    def _(s):
        gone(sibr.at[0], s_sb.at[s])

    @pl.loop(0, 6)
    def _(s):
        for half in range(2):
            gone(xr.at[0, pl.ds(0, HALF)], s_x.at[s, half])

    @pl.loop(1, NE)
    def _(d):
        s = (e + d) % NE

        @pl.when(e < 7)
        def _():
            gone(w2s.at[0], s_w2.at[s])

        gone(b1s.at[0], s_b1.at[s])
        gone(b2s.at[0], s_b2.at[s])
        gone(ps.at[0], s_e.at[s])

    @pl.loop(1, 4)
    def _(d):
        t = (z + d) % 4
        for half in range(2):
            gone(cp.at[0, 0], s_c.at[half, t])
            for k in range(4):
                gone(tp.at[0, 0, 0], s_t.at[k, half, t])

    raw_routes.wait_send()
    raw_cot.wait_send()
    for k in range(4):
        raw(k).wait_send()


def body(tokens, routes, cotangent, weights, first_moment, second_moment, pairing):
    dma = pltpu.SemaphoreType.DMA
    vmem = pl.BlockSpec(memory_space=pltpu.VMEM)
    hbm = pl.BlockSpec(memory_space=pl.ANY)
    act, wn, m1n, m2n, g = pl.pallas_call(
        kernel,
        out_shape=(
            jax.ShapeDtypeStruct((TOK, 2, FW), BF),
            jax.ShapeDtypeStruct((SHARD, FW), BF),
            jax.ShapeDtypeStruct((SHARD, FW), BF),
            jax.ShapeDtypeStruct((SHARD, FW), BF),
            jax.ShapeDtypeStruct((SHARD, FW), F32),
        ),
        in_specs=[pl.BlockSpec(memory_space=pltpu.SMEM), vmem, vmem, vmem, vmem, hbm, hbm],
        out_specs=(vmem,) * 5,
        scratch_shapes=[
            pltpu.VMEM((NE, 32, FW), BF),
            pltpu.VMEM((NE, 32, FW), BF),
            pltpu.VMEM((16, SHARD, FW), BF),
            pltpu.VMEM((NE, 112, 640), BF),
            pltpu.VMEM((NE, 112, 640), BF),
            pltpu.VMEM((NE, 112, 640), BF),
            pltpu.VMEM((NE, 112, 640), BF),
            pltpu.VMEM((4, 2, 4, CAP, CHUNK), BF),
            pltpu.VMEM((4, NE, CAP, CHUNK), BF),
            pltpu.VMEM((2, 4, CAP, FW), BF),
            pltpu.VMEM((NE, CAP, FW), BF),
            pltpu.VMEM((ROWS, FW), F32),
            pltpu.VMEM((NE, CAP, FW), BF),
            pltpu.VMEM((NE, CAP, FW), BF),
            pltpu.VMEM((16, SHARD, FW), BF),
            pltpu.VMEM((NE, SHARD, FW), BF),
            pltpu.VMEM((6, SHARD, FW), BF),
            pltpu.VMEM((SHARD, FW), BF),
            pltpu.VMEM((ROWS, TOK), BF),
            pltpu.VMEM((ROWS, TOK), BF),
            pltpu.VMEM((2, TOK), jnp.int32),
            pltpu.VMEM((4, TOK, CHUNK), BF),
            pltpu.VMEM((TOK, 2, FW), BF),
            pltpu.VMEM((2, ROWS // 2, TOK), BF),
            pltpu.VMEM((2, ROWS // 2, TOK), BF),
            dma((2,)),
            dma((NE,)), dma((NE,)), dma((NE,)), dma((NE,)),
            dma((NE,)), dma((NE,)), dma((NE,)), dma((NE,)),
            dma((4, 2, 4)), dma((4, NE)),
            dma((2, 4)), dma((NE,)), dma((NE,)), dma((NE,)),
            dma((15,)), dma((16,)),
            dma((NE,)), dma((NE,)),
            dma((6, 2)), dma((6, 2)),
            dma((2,)), dma((2,)),
            dma((6,)), dma((6,)),
        ],
        compiler_params=pltpu.CompilerParams(
            collective_id=0, has_side_effects=True, vmem_limit_bytes=63 * 1024 * 1024
        ),
    )(
        pairing,
        routes.T,
        tokens,
        cotangent,
        weights.reshape(SHARD, FW),
        first_moment.reshape(SHARD, FW),
        second_moment.reshape(SHARD, FW),
    )
    new_first = BETA_ONE * m1n.astype(F32) + (1.0 - BETA_ONE) * g
    new_second = BETA_TWO * m2n.astype(F32) + (1.0 - BETA_TWO) * g * g
    update = new_first / (jnp.sqrt(new_second) + EPSILON)
    shape = first_moment.shape
    return (
        act,
        wn.reshape(weights.shape),
        new_first.reshape(shape),
        new_second.reshape(shape),
        update.reshape(shape),
    )


def solution(mesh):
    in_specs = (
        P(("expert", "replica"), None),
        P(("expert", "replica"), None),
        P(("expert", "replica"), None, None),
        P("expert", "replica", None),
        P("expert", "replica", None),
        P("expert", "replica", None),
        P(),
    )
    out_specs = (
        P(("expert", "replica"), None, None),
        P("expert", "replica", None),
        P("expert", "replica", None),
        P("expert", "replica", None),
        P("expert", "replica", None),
    )
    return jax.shard_map(body, mesh=mesh, in_specs=in_specs, out_specs=out_specs, check_vma=False)
```
